256 devices in a mesh: section: 4 (over z_lo), seq: 64 (over x, y, z_hi, core).
Axes of the slice: x: 4, y: 4, z: 8 (z_hi: 2, z_lo: 4; z = z_hi * 4 + z_lo), core: 2. Of those that a mesh axis runs over, the one named last changes fastest.
Arguments:
- tokens: bfloat16 [65536, 1024], P('seq'), may hold values from -8 to 8
- enc_gain: float32 [1024], replicated, may hold values from 0.1 to 1.9
- w_query: bfloat16 [1024, 1024], P(None, 'section'), may hold values from -8 to 8
- w_key: bfloat16 [1024, 1024], P(None, 'section'), may hold values from -8 to 8
- w_value: bfloat16 [1024, 1024], P(None, 'section'), may hold values from -0.1875 to 0.1875
- w_out: bfloat16 [1024, 1024], P('section'), may hold values from -0.1875 to 0.1875
- neighbours: int32 [512, 8], P('seq'), may hold values from 0 to 511, as said below
- counts: int32 [512], P('seq'), may hold values from 3 to 8, as said below
- stain_of_section: int32 [4], P('section'), may hold values from 0 to 2, as said below
- stain_gain: float32 [3, 1024], replicated, may hold values from 0.1 to 1.9
- stain_weight: bfloat16 [3, 1024, 768], replicated, may hold values from -0.1875 to 0.1875
Outputs:
- patches: bfloat16 [4, 65536, 768], P('section', 'seq')
The draws below stay inside these ranges and needn't reach their ends.
Inputs may be any that keep to these rules, and one draw needn't show every extreme that they name: neighbours[i, j] names a block held by the same index of seq as block i or by the index before or after it; slot 0 is block i itself, slot 1 a block of the index before (block 0 on the first), slot 2 a block of the index after (the last block on the last). `counts`: some block uses all 8 slots. `stain_of_section`: every stain is named by some section.
All inputs are finite; a program needn't handle non-finite values.
Results may differ from the reference program's by a relative error of at most 0.019.
Values may be sent and summed in bfloat16 or wider, within the bound.
A program may use at most 128 MiB of HBM per device.

```python
import jax
import jax.numpy as jnp
from jax import lax

D = 1024
HEADS = 16
HEAD_DIM = 64
PIX = 768
STAINS = 3
BLOCK = 128
NEIGH = 8
TOK_DEV = 1024
TOKENS = 65536
NBLK = 512
N_SECTION = 4
N_SEQ = 64


def draw_tokens(key, part):
    key = jax.random.fold_in(key, 23)
    first = jax.random.fold_in(key, 0)
    base = jax.random.normal(first, (TOKENS, D), jnp.float32)
    return jnp.clip(base, -8.0, 8.0).astype(jnp.bfloat16)


def draw_w_query(key, part):
    key = jax.random.fold_in(key, 21)
    own = jax.random.normal(key, (D, D), jnp.float32) * D ** (-0.5)
    drawn = own
    return jnp.clip(drawn, -8.0, 8.0).astype(jnp.bfloat16)


def draw_w_key(key, part):
    key = jax.random.fold_in(key, 22)
    own = jax.random.normal(key, (D, D), jnp.float32) * D ** (-0.5)
    drawn = own
    return jnp.clip(drawn, -8.0, 8.0).astype(jnp.bfloat16)


def draw_neighbours(key, part):
    key = jax.random.fold_in(key, 11)
    first, second, third = jax.random.split(key, 3)
    per_dev = TOK_DEV // BLOCK
    rows = jnp.arange(NBLK, dtype=jnp.int32)
    owner = rows // per_dev
    lowest = jnp.maximum(owner - 1, 0) * per_dev
    highest = jnp.minimum(owner + 2, N_SEQ) * per_dev
    spread = jax.random.randint(first, (NBLK, NEIGH), lowest[:, None], highest[:, None])
    before = jax.random.randint(second, (NBLK,), lowest, jnp.maximum(owner * per_dev, lowest + 1))
    after = jax.random.randint(third, (NBLK,), jnp.minimum((owner + 1) * per_dev, highest - 1), highest)
    spread = spread.at[:, 0].set(rows).at[:, 1].set(before).at[:, 2].set(after)
    return spread.astype(jnp.int32)


def draw_counts(key, part):
    key = jax.random.fold_in(key, 12)
    used = jax.random.randint(key, (NBLK,), 3, NEIGH + 1)
    return used.at[0].set(NEIGH).astype(jnp.int32)


def draw_stain_of_section(key, part):
    key = jax.random.fold_in(key, 13)
    first, second = jax.random.split(key)
    order = jax.random.permutation(first, STAINS)
    extra = jax.random.randint(second, (N_SECTION - STAINS,), 0, STAINS)
    return jnp.concatenate([order, extra]).astype(jnp.int32)


def shard_levels(rng, dims, cuts, least, top_value):
    def one(axis_at, shards_of):
        steps = jax.random.uniform(jax.random.fold_in(jax.random.fold_in(rng, 6), axis_at), (shards_of,), jnp.float32, least / len(cuts), top_value / len(cuts))
        return jnp.repeat(jnp.exp(steps), dims[axis_at] // shards_of).reshape((-1,) + (1,) * (len(dims) - axis_at - 1))

    level = one(*cuts[0])
    for cut in cuts[1:]:
        level = level * one(*cut)
    return level


def centred(stream_key, shape, deviation, reach, pieces=(), kind=jnp.bfloat16):
    level = shard_levels(stream_key, shape, pieces, -0.22, 0.18) if pieces else 1.0
    entries = jax.random.normal(stream_key, shape, jnp.float32) * deviation * level
    return jnp.minimum(jnp.maximum(entries, -reach), reach).astype(kind)


def setup_inputs(seed: int = 0) -> dict:
    key_of = jax.random.split(jax.random.key(seed), 12)
    return {
        "tokens": draw_tokens(jax.random.fold_in(key_of[11], 71), 0),
        "enc_gain": jnp.clip(1.0 + 0.18 * jax.random.normal(key_of[1], (D,), jnp.float32), 0.1, 1.9),
        "w_query": draw_w_query(jax.random.fold_in(key_of[11], 71), 0),
        "w_key": draw_w_key(jax.random.fold_in(key_of[11], 71), 0),
        "w_value": centred(key_of[4], (D, D), D ** -0.5, 0.1875, ((1, 4),)),
        "w_out": centred(key_of[5], (D, D), D ** -0.5, 0.1875, ((0, 4),)),
        "neighbours": draw_neighbours(jax.random.fold_in(key_of[11], 71), 0),
        "counts": draw_counts(jax.random.fold_in(key_of[11], 71), 0),
        "stain_of_section": draw_stain_of_section(jax.random.fold_in(key_of[11], 71), 0),
        "stain_gain": jnp.clip(1.0 + 0.18 * jax.random.normal(key_of[9], (STAINS, D), jnp.float32), 0.1, 1.9),
        "stain_weight": centred(key_of[10], (STAINS, D, PIX), D ** -0.5, 0.1875),
    }


def rms_norm(values, gain):
    values = values.astype(jnp.float32)
    return values * lax.rsqrt(lax.optimization_barrier(jnp.mean(values * values, axis=-1, keepdims=True)) + 1e-05) * gain

def reference(tokens, enc_gain, w_query, w_key, w_value, w_out, neighbours, counts, stain_of_section, stain_gain, stain_weight):
    normed = rms_norm(tokens, enc_gain).astype(jnp.bfloat16)
    queries = jnp.dot(normed, w_query, preferred_element_type=jnp.float32).astype(jnp.bfloat16)
    keys = jnp.dot(normed, w_key, preferred_element_type=jnp.float32).astype(jnp.bfloat16)
    values = jnp.dot(normed, w_value, preferred_element_type=jnp.float32).astype(jnp.bfloat16)
    key_blocks = keys.reshape(NBLK, BLOCK, HEADS, HEAD_DIM)
    value_blocks = values.reshape(NBLK, BLOCK, HEADS, HEAD_DIM)
    query_blocks = queries.reshape(NBLK, BLOCK, HEADS, HEAD_DIM)

    def one_block(items):
        query_block, listed, used = items
        near_keys = key_blocks[listed].reshape(NEIGH * BLOCK, HEADS, HEAD_DIM).astype(jnp.float32)
        near_values = value_blocks[listed].reshape(NEIGH * BLOCK, HEADS, HEAD_DIM).astype(jnp.float32)
        scores = jnp.einsum('qhd,khd->hqk', query_block.astype(jnp.float32), near_keys) * 0.125
        valid = jnp.arange(NEIGH * BLOCK, dtype=jnp.int32) // BLOCK < used
        scores = jnp.where(valid[None, None, :], scores, -1e+30)
        top = lax.optimization_barrier(jnp.max(scores, axis=-1, keepdims=True))
        expo = jnp.exp(scores - top)
        weights = (expo / lax.optimization_barrier(jnp.sum(expo, axis=-1, keepdims=True))).astype(jnp.bfloat16)
        return jnp.einsum('hqk,khd->qhd', weights.astype(jnp.float32), near_values).astype(jnp.bfloat16)
    attended = lax.map(one_block, (query_blocks, neighbours, counts)).reshape(TOKENS, D)
    encoded = (tokens.astype(jnp.float32) + jnp.dot(attended, w_out, preferred_element_type=jnp.float32)).astype(jnp.bfloat16)
    results = []
    for section_num in range(N_SECTION):
        stain = stain_of_section[section_num]
        decoded = rms_norm(encoded, stain_gain[stain]).astype(jnp.bfloat16)
        results.append(jnp.dot(decoded, stain_weight[stain], preferred_element_type=jnp.float32).astype(jnp.bfloat16))
    return jnp.stack(results)
```

```python
import functools

import jax
import jax.numpy as jnp
from jax import lax
from jax.experimental import pallas as pl
from jax.experimental.pallas import tpu as pltpu
from jax.sharding import PartitionSpec as P

HEAD_DIM = 64
BLOCK = 128
NEIGH = 8
TOK = 1024
WIDTH = 1024
PIX = 768
GROUP = 4
COLS = WIDTH // GROUP
CHUNK = 32
HALF = TOK // 2
CHUNKS = HALF // CHUNK
STEPS = CHUNKS + GROUP - 1
QSCALE = 0.125 * 1.4426950408889634

F32 = jnp.float32
BF16 = jnp.bfloat16
MESH = pl.DeviceIdType.MESH


def gather_project(
    tok_hbm, gain_ref, wq_hbm, wk_hbm, wv_hbm, wo_hbm,
    q_out, kv_out, wo_out,
    raw, norm, wts, q_buf, own_kv, halo_kv,
    tok_sem, wload_sem, lo_send, lo_recv, hi_send, hi_recv,
    z_send, z_recv, row_send, row_recv, col_send, col_recv, pair_send, pair_recv,
    kv_send, kv_recv, store_sem, hstore_sem,
):
    sec = lax.axis_index("section")
    seq = lax.axis_index("seq")
    core = seq % 2
    zhi = (seq // 2) % 2
    yy = (seq // 4) % 4
    xx = seq // 16
    u = xx * (1 - core) + yy * core
    v = yy * (1 - core) + xx * core

    def seq_at(u1, v1):
        x1 = u1 * (1 - core) + v1 * core
        y1 = v1 * (1 - core) + u1 * core
        return ((x1 * 4 + y1) * 2 + zhi) * 2 + core

    def z_at(step):
        z1 = (zhi * 4 + sec + step + 8) % 8
        return (z1 % 4, seq + (z1 // 4 - zhi) * 2)

    sibling = (sec, seq + 1 - 2 * core)
    partner = (seq + 2 * core - 1 + 64) % 64
    up, down = z_at(1), z_at(7)
    two_up, two_down = z_at(2), z_at(6)
    first = jnp.where(sec == 0, 1, 0)
    last = jnp.where(sec == 3, 1, 0)
    lo_to = ((sec + 3) % 4, jnp.where(sec == 0, partner, seq))
    hi_to = ((sec + 1) % 4, jnp.where(sec == 3, partner, seq))
    row_to = [(sec, seq_at((u + d) % 4, v)) for d in (1, 3, 2)]
    col_to = [(sec, seq_at(u, (v + d) % 4)) for d in (1, 3)]

    tok_loads = []
    for i in range(4):
        rows = pl.ds(i * 256, 256)
        tok_loads.append(pltpu.make_async_copy(tok_hbm.at[rows, :], raw.at[rows, :], tok_sem.at[i]))
    w_loads = [
        pltpu.make_async_copy(src, wts.at[0, i], wload_sem.at[i])
        for i, src in enumerate((wq_hbm, wk_hbm, wv_hbm))
    ]
    for i in range(4):
        w_loads.append(
            pltpu.make_async_copy(
                wo_hbm.at[:, pl.ds(i * COLS, COLS)],
                wts.at[0, 3, pl.ds(i * COLS, COLS), :],
                wload_sem.at[3 + i],
            )
        )
    for copy in tok_loads + w_loads:
        copy.start()

    barrier = pltpu.get_barrier_semaphore()
    peers = [sibling, up, down, two_up, two_down, lo_to, hi_to] + row_to + col_to
    for peer in peers:
        pl.semaphore_signal(barrier, inc=1, device_id=peer, device_id_type=MESH)

    gain = gain_ref[...]
    for i in range(4):
        tok_loads[i].wait()

        def norm_rows(t, _):
            rows = pl.ds(pl.multiple_of(i * 256 + t * 128, 128), 128)
            x = raw[rows, :].astype(F32)
            scale = lax.rsqrt(jnp.mean(x * x, axis=-1, keepdims=True) + 1e-05)
            norm[0, rows, :] = (x * scale * gain).astype(BF16)
            return 0

        lax.fori_loop(0, 2, norm_rows, 0)

    pl.semaphore_wait(barrier, len(peers))

    def remote(src, dst, send, recv, to):
        return pltpu.make_async_remote_copy(
            src_ref=src, dst_ref=dst, send_sem=send, recv_sem=recv, device_id=to, device_id_type=MESH
        )

    def lo_copy(j):
        rows = pl.ds(pl.multiple_of(j * CHUNK, CHUNK), CHUNK)
        return remote(norm.at[1 - first, rows, :], norm.at[1, rows, :], lo_send.at[j], lo_recv.at[j], lo_to)

    def hi_copy(j):
        rows = pl.ds(pl.multiple_of(HALF + j * CHUNK, CHUNK), CHUNK)
        return remote(norm.at[1 - last, rows, :], norm.at[1, rows, :], hi_send.at[j], hi_recv.at[j], hi_to)

    def start_lo(j, _):
        lo_copy(j).start()
        return 0

    def start_hi(j, _):
        hi_copy(j).start()
        return 0

    piece = pl.ds(pl.multiple_of(core * HALF + (v * 4 + u) * 32, 32), 32)

    def slab(g, rows):
        if g < 3:
            return wts.at[g + 1, pl.ds(0, 3), rows, :]
        return wts.at[pl.ds(1, 3), 3, rows, :]

    two_sec = jnp.where(core == 0, two_up[0], two_down[0])
    two_seq = jnp.where(core == 0, two_up[1], two_down[1])
    z_to = [down, (two_sec, two_seq), up]
    z_copies = [
        remote(wts.at[0, pl.ds(0, 3), piece, :], wts.at[r + 1, pl.ds(0, 3), piece, :], z_send.at[r], z_recv.at[r], z_to[r])
        for r in range(3)
    ] + [
        remote(wts.at[0, 3, piece, :], wts.at[r + 1, 3, piece, :], z_send.at[3 + r], z_recv.at[3 + r], z_to[r])
        for r in range(3)
    ]
    for copy in w_loads:
        copy.wait()
    for copy in z_copies:
        copy.start()

    @pl.when(sec == 0)
    def _():
        lax.fori_loop(0, CHUNKS, start_lo, 0)

    @pl.when(sec == 3)
    def _():
        lax.fori_loop(0, CHUNKS, start_hi, 0)

    def row_copy(g, d):
        return remote(slab(g, piece), slab(g, piece), row_send.at[g * 3 + d], row_recv.at[g * 3 + d], row_to[d])

    def set_rows(v1, start=0, size=128):
        return pl.ds(pl.multiple_of(core * HALF + v1 * 128 + start, 32), size)

    def col_copy(g, d):
        if d < 2:
            rows = set_rows(v)
        elif d == 2:
            rows = set_rows((v + 3) % 4, 0, 64)
        else:
            rows = set_rows((v + 1) % 4, 64, 64)
        return remote(slab(g, rows), slab(g, rows), col_send.at[g * 4 + d], col_recv.at[g * 4 + d], col_to[d % 2])

    def pair_copy(g, d):
        rows = set_rows((v + d) % 4)
        return remote(slab(g, rows), slab(g, rows), pair_send.at[g * 4 + d], pair_recv.at[g * 4 + d], sibling)

    def e1(g):
        if g < 3:
            z_copies[g].wait_recv()
        else:
            for r in range(3):
                z_copies[3 + r].wait_recv()
        for d in range(3):
            row_copy(g, d).start()

    def e3(g):
        for d in range(3):
            row_copy(g, d).wait_recv()
        for d in range(2):
            col_copy(g, d).start()
        pair_copy(g, 0).start()

    def e4(g):
        col_copy(g, 0).wait_recv()
        col_copy(g, 2).start()
        pair_copy(g, 3).start()
        col_copy(g, 1).wait_recv()
        col_copy(g, 3).start()
        pair_copy(g, 1).start()

    def e5(g):
        col_copy(g, 2).wait_recv()
        col_copy(g, 3).wait_recv()
        pair_copy(g, 2).start()

    def e6(g):
        for d in range(4):
            pair_copy(g, d).wait_recv()

    def halo_step(k):
        j = k - 3 + sec

        @pl.when((j >= 0) & (j < CHUNKS))
        def _():
            lo_copy(j).wait_recv()

            @pl.when(sec != 0)
            def _():
                lo_copy(j).start()

        i = k - sec

        @pl.when((i >= 0) & (i < CHUNKS))
        def _():
            hi_copy(i).wait_recv()

            @pl.when(sec != 3)
            def _():
                hi_copy(i).start()

    def own_unit(r, t):
        rows = pl.ds(pl.multiple_of(t * 256, 256), 256)
        x = norm[0, rows, :]
        q = jnp.dot(x, wts[r, 0], preferred_element_type=F32)
        q_buf[r, rows, :] = (q * QSCALE).astype(BF16)
        own_kv[r, 0, rows, :] = jnp.dot(x, wts[r, 1], preferred_element_type=F32).astype(BF16)
        own_kv[r, 1, rows, :] = jnp.dot(x, wts[r, 2], preferred_element_type=F32).astype(BF16)

    def halo_unit(m, r):
        low = pl.ds(pl.multiple_of(m * 128, 128), 128)
        high = pl.ds(pl.multiple_of(HALF + m * 128, 128), 128)
        x = jnp.concatenate([norm[1, low, :], norm[1, high, :]], axis=0)
        for w in range(2):
            y = jnp.dot(x, wts[r, 1 + w], preferred_element_type=F32).astype(BF16)
            halo_kv[w, r, low, :] = y[:128]
            halo_kv[w, r, high, :] = y[128:]

    def own_stores(r):
        return [
            pltpu.make_async_copy(q_buf.at[r], q_out.at[r], store_sem.at[r * 2]),
            pltpu.make_async_copy(own_kv.at[r], kv_out.at[:, r, pl.ds(0, TOK), :], store_sem.at[r * 2 + 1]),
        ]

    def kv_copy(r):
        return remote(own_kv.at[r], kv_out.at[:, r, pl.ds(2 * TOK, TOK), :], kv_send.at[r], kv_recv.at[r], sibling)

    def halo_stores(m):
        copies = []
        for h in range(2):
            copies.append(
                pltpu.make_async_copy(
                    halo_kv.at[:, :, pl.ds(h * HALF + m * 128, 128), :],
                    kv_out.at[:, :, pl.ds(TOK + h * HALF + m * 128, 128), :],
                    hstore_sem.at[m * 2 + h],
                )
            )
        return copies

    def finish_own(r):
        for copy in own_stores(r):
            copy.start()
        kv_copy(r).start()

    def run(first_step, last_step, events, unit):
        def body(k, _):
            halo_step(k)
            for at, event in events:
                pl.when(k == at)(event)
            unit(k)
            return 0

        lax.fori_loop(first_step, last_step + 1, body, 0)

    def seqn(*pairs):
        def go():
            for fn, g in pairs:
                fn(g)

        return go

    run(0, 3, [(1, seqn((e1, 0), (e1, 1))), (2, seqn((e1, 2), (e1, 3))), (3, seqn((e3, 0)))], lambda k: own_unit(0, k))
    finish_own(0)
    run(4, 6, [(4, seqn((e3, 1), (e3, 2))), (5, seqn((e3, 3), (e4, 0))), (6, seqn((e5, 0)))], lambda k: None)

    def unit_r1(k):
        own_unit(1, k - 7)

        @pl.when(k < 9)
        def _():
            halo_unit(0, k - 7)

    run(7, 10, [(7, seqn((e6, 0))), (8, seqn((e4, 1))), (9, seqn((e5, 1)))], unit_r1)
    finish_own(1)

    def unit_r2(k):
        own_unit(2, k - 11)
        t = k - 11
        halo_unit(1 - t // 3, t - t // 3)

    run(11, 14, [(11, seqn((e6, 1), (e4, 2))), (12, seqn((e5, 2))), (13, seqn((e4, 3))), (14, seqn((e5, 3)))], unit_r2)
    finish_own(2)

    def unit_r3(k):
        own_unit(3, k - 15)
        halo_unit(2, k - 15)

        @pl.when(k < 17)
        def _():
            halo_unit(k - 15, 3)

    run(15, STEPS - 1, [(15, seqn((e6, 2))), (16, seqn((e6, 3)))], unit_r3)
    finish_own(3)
    wo_store = pltpu.make_async_copy(wts.at[:, 3], wo_out, wload_sem.at[7])
    wo_store.start()
    for m in range(3):
        for copy in halo_stores(m):
            copy.start()

    def tail(r, _):
        halo_unit(3, r)
        return 0

    lax.fori_loop(0, GROUP, tail, 0)
    for copy in halo_stores(3):
        copy.start()

    def drain(j, _):
        lo_copy(j).wait_send()
        hi_copy(j).wait_send()
        return 0

    lax.fori_loop(0, CHUNKS, drain, 0)
    for copy in z_copies:
        copy.wait_send()
    for g in range(4):
        for d in range(3):
            row_copy(g, d).wait_send()
        for d in range(4):
            col_copy(g, d).wait_send()
            pair_copy(g, d).wait_send()
    for r in range(GROUP):
        for copy in own_stores(r):
            copy.wait()
        kv_copy(r).wait()
    wo_store.wait()
    for m in range(4):
        for copy in halo_stores(m):
            copy.wait()


def project(tokens, gain, wq, wk, wv, wo):
    any_spec = pl.BlockSpec(memory_space=pl.ANY)
    dma = pltpu.SemaphoreType.DMA
    return pl.pallas_call(
        gather_project,
        out_shape=[
            jax.ShapeDtypeStruct((GROUP, TOK, COLS), BF16),
            jax.ShapeDtypeStruct((2, GROUP, 3 * TOK, COLS), BF16),
            jax.ShapeDtypeStruct((GROUP, WIDTH, COLS), BF16),
        ],
        in_specs=[any_spec, pl.BlockSpec(memory_space=pltpu.VMEM)] + [any_spec] * 4,
        out_specs=[any_spec] * 3,
        scratch_shapes=[
            pltpu.VMEM((TOK, WIDTH), BF16),
            pltpu.VMEM((2, TOK, WIDTH), BF16),
            pltpu.VMEM((GROUP, 4, WIDTH, COLS), BF16),
            pltpu.VMEM((GROUP, TOK, COLS), BF16),
            pltpu.VMEM((GROUP, 2, TOK, COLS), BF16),
            pltpu.VMEM((2, GROUP, TOK, COLS), BF16),
            dma((4,)), dma((8,)),
            dma((CHUNKS,)), dma((CHUNKS,)), dma((CHUNKS,)), dma((CHUNKS,)),
            dma((6,)), dma((6,)), dma((12,)), dma((12,)), dma((16,)), dma((16,)), dma((16,)), dma((16,)),
            dma((4,)), dma((4,)), dma((8,)), dma((8,)),
        ],
        compiler_params=pltpu.CompilerParams(
            collective_id=0, has_side_effects=True, vmem_limit_bytes=52 * 2**20
        ),
        name="gather_project",
    )(tokens, gain, wq, wk, wv, wo)


PAIRS = 4


def attend_decode(
    ids_ref, counts_ref, stain_ref,
    q_ref, k_ref, v_ref, wo_ref, tok_ref, gain_ref, sw_ref,
    out_ref, att, e_scr,
):
    del stain_ref
    step = pl.program_id(0)
    lane = lax.broadcasted_iota(jnp.int32, (BLOCK, BLOCK), 1)

    def block(i, _):
        rows = pl.ds(pl.multiple_of(i * BLOCK, BLOCK), BLOCK)
        starts = [pl.multiple_of(ids_ref[i, j] * BLOCK, BLOCK) for j in range(NEIGH)]

        def run(n):
            for p in range(PAIRS):
                r, c = p // 2, (p % 2) * BLOCK
                q = q_ref[r, rows, c : c + BLOCK]
                zero = jnp.zeros_like(q)
                both = jnp.concatenate([jnp.where(lane < HEAD_DIM, q, zero), jnp.where(lane < HEAD_DIM, zero, q)], axis=0)
                k = jnp.concatenate([k_ref[0, r, pl.ds(starts[j], BLOCK), c : c + BLOCK] for j in range(n)], axis=0)
                s = lax.dot_general(both, k, (((1,), (1,)), ((), ())), preferred_element_type=F32)
                top = jnp.max(s, axis=1, keepdims=True)
                e_scr[p, :, : n * BLOCK] = jnp.exp2(s - top).astype(BF16)
            for p in range(PAIRS):
                r, c = p // 2, (p % 2) * BLOCK
                v = jnp.concatenate([v_ref[0, r, pl.ds(starts[j], BLOCK), c : c + BLOCK] for j in range(n)], axis=0)
                v = jnp.concatenate([v, jnp.ones((n * BLOCK, BLOCK), BF16)], axis=1)
                o = jnp.dot(e_scr[p, :, : n * BLOCK], v, preferred_element_type=F32)
                o = o[:, :BLOCK] / o[:, BLOCK:]
                att[step * 2 + r, rows, c : c + BLOCK] = jnp.where(lane < HEAD_DIM, o[:BLOCK], o[BLOCK:]).astype(BF16)

        for n in range(3, NEIGH + 1):
            pl.when(counts_ref[i] == n)(functools.partial(run, n))
        return 0

    lax.fori_loop(0, TOK // BLOCK, block, 0)

    @pl.when(step == GROUP // 2 - 1)
    def _():
        gain = gain_ref[0]

        def rows_out(t, _):
            rows = pl.ds(pl.multiple_of(t * 256, 256), 256)
            x = jnp.concatenate([att[r, rows, :] for r in range(GROUP)], axis=1)
            parts = []
            for c in range(GROUP):
                w = jnp.concatenate([wo_ref[r, c * COLS : (c + 1) * COLS, :] for r in range(GROUP)], axis=0)
                parts.append(jnp.dot(x, w, preferred_element_type=F32))
            mixed = jnp.concatenate(parts, axis=1)
            encoded = (tok_ref[rows, :].astype(F32) + mixed).astype(BF16).astype(F32)
            scale = lax.rsqrt(jnp.mean(encoded * encoded, axis=-1, keepdims=True) + 1e-05)
            decoded = (encoded * scale * gain).astype(BF16)
            out_ref[0, rows, :] = jnp.dot(decoded, sw_ref[0], preferred_element_type=F32).astype(BF16)
            return 0

        lax.fori_loop(0, 4, rows_out, 0)


def attention(ids, counts, stain, q, kv, wo, tokens, stain_gain, stain_weight):
    half = GROUP // 2
    return pl.pallas_call(
        attend_decode,
        out_shape=jax.ShapeDtypeStruct((1, TOK, PIX), BF16),
        grid_spec=pltpu.PrefetchScalarGridSpec(
            num_scalar_prefetch=3,
            grid=(2,),
            in_specs=[
                pl.BlockSpec((half, TOK, COLS), lambda g, *_: (g, 0, 0)),
                pl.BlockSpec((1, half, 3 * TOK, COLS), lambda g, *_: (0, g, 0, 0)),
                pl.BlockSpec((1, half, 3 * TOK, COLS), lambda g, *_: (1, g, 0, 0)),
                pl.BlockSpec((GROUP, WIDTH, COLS), lambda g, *_: (0, 0, 0), pipeline_mode=pl.Buffered(1)),
                pl.BlockSpec((TOK, WIDTH), lambda g, *_: (0, 0), pipeline_mode=pl.Buffered(1)),
                pl.BlockSpec((1, 1, WIDTH), lambda g, ids, counts, stain: (stain[0], 0, 0)),
                pl.BlockSpec((1, WIDTH, PIX), lambda g, ids, counts, stain: (stain[0], 0, 0), pipeline_mode=pl.Buffered(1)),
            ],
            out_specs=pl.BlockSpec((1, TOK, PIX), lambda g, *_: (0, 0, 0)),
            scratch_shapes=[
                pltpu.VMEM((GROUP, TOK, COLS), BF16),
                pltpu.VMEM((PAIRS, 2 * BLOCK, NEIGH * BLOCK), BF16),
            ],
        ),
        compiler_params=pltpu.CompilerParams(vmem_limit_bytes=56 * 2**20),
        name="attend_decode",
    )(ids, counts, stain, q, kv, kv, wo, tokens, stain_gain[:, None, :], stain_weight)


def per_device(
    tokens, enc_gain, w_query, w_key, w_value, w_out, neighbours, counts, stain_of_section, stain_gain, stain_weight
):
    q, kv, wo = project(tokens, enc_gain[None, :], w_query, w_key, w_value, w_out)
    seq = lax.axis_index("seq")
    blocks = TOK // BLOCK
    owner = neighbours // blocks - seq
    chip_side = 2 * (seq % 2) - 1
    part = jnp.where(owner == 0, 0, jnp.where(owner == chip_side, 1, 2))
    ids = part * blocks + neighbours % blocks
    return attention(ids, counts, stain_of_section, q, kv, wo, tokens, stain_gain, stain_weight)


def solution(mesh):
    placed = (
        P("seq", None),
        P(),
        P(None, "section"),
        P(None, "section"),
        P(None, "section"),
        P("section", None),
        P("seq", None),
        P("seq"),
        P("section"),
        P(),
        P(),
    )
    return jax.shard_map(
        per_device, mesh=mesh, in_specs=placed, out_specs=P("section", "seq", None), check_vma=False
    )
```

```python
import functools

import jax
import jax.numpy as jnp
from jax import lax
from jax.experimental import pallas as pl
from jax.experimental.pallas import tpu as pltpu
from jax.sharding import PartitionSpec as P

HEAD_DIM = 64
BLOCK = 128
NEIGH = 8
TOK = 1024
WIDTH = 1024
PIX = 768
GROUP = 4
COLS = WIDTH // GROUP
CHUNK = 16
HALF = TOK // 2
CHUNKS = HALF // CHUNK
SKEW = 5
AHEAD = 6
STEPS = CHUNKS + SKEW * (GROUP - 1)
QSCALE = 0.125 * 1.4426950408889634

F32 = jnp.float32
BF16 = jnp.bfloat16
MESH = pl.DeviceIdType.MESH


def gather_project(
    tok_hbm, gain_hbm, wq_hbm, wk_hbm, wv_hbm, wo_hbm,
    q_out, kv_out, wo_out,
    gain_buf, raw, norm, wts, q_buf, own_kv, halo_kv,
    gain_sem, tok_sem, wload_sem, lo_send, lo_recv, hi_send, hi_recv,
    z_send, z_recv, row_send, row_recv, col_send, col_recv, pair_send, pair_recv,
    kv_send, kv_recv, store_sem, hstore_sem,
):
    sec = lax.axis_index("section")
    seq = lax.axis_index("seq")
    core = seq % 2
    zhi = (seq // 2) % 2
    yy = (seq // 4) % 4
    xx = seq // 16
    u = xx * (1 - core) + yy * core
    v = yy * (1 - core) + xx * core

    def seq_at(u1, v1):
        x1 = u1 * (1 - core) + v1 * core
        y1 = v1 * (1 - core) + u1 * core
        return ((x1 * 4 + y1) * 2 + zhi) * 2 + core

    def z_at(step):
        z1 = (zhi * 4 + sec + step + 8) % 8
        return (z1 % 4, seq + (z1 // 4 - zhi) * 2)

    sibling = (sec, seq + 1 - 2 * core)
    partner = (seq + 2 * core - 1 + 64) % 64
    up, down = z_at(1), z_at(7)
    two_up, two_down = z_at(2), z_at(6)
    first = jnp.where(sec == 0, 1, 0)
    last = jnp.where(sec == 3, 1, 0)
    lo_to = ((sec + 3) % 4, jnp.where(sec == 0, partner, seq))
    hi_to = ((sec + 1) % 4, jnp.where(sec == 3, partner, seq))
    row_to = [(sec, seq_at((u + d) % 4, v)) for d in (1, 3)]
    col_to = [(sec, seq_at(u, (v + d) % 4)) for d in (1, 3)]

    tok_loads = []
    for i in range(4):
        rows = pl.ds(i * 256, 256)
        tok_loads.append(pltpu.make_async_copy(tok_hbm.at[rows, :], raw.at[0, rows, :], tok_sem.at[i]))
    w_loads = [
        pltpu.make_async_copy(src, wts.at[0, i], wload_sem.at[i])
        for i, src in enumerate((wq_hbm, wk_hbm, wv_hbm))
    ]
    for i in range(4):
        w_loads.append(
            pltpu.make_async_copy(
                wo_hbm.at[:, pl.ds(i * COLS, COLS)],
                wts.at[0, 3, pl.ds(i * COLS, COLS), :],
                wload_sem.at[3 + i],
            )
        )
    gain_load = pltpu.make_async_copy(gain_hbm, gain_buf, gain_sem)
    for copy in [gain_load] + tok_loads + w_loads:
        copy.start()

    barrier = pltpu.get_barrier_semaphore()
    peers = [sibling, up, down, two_up, two_down, lo_to, hi_to] + row_to + col_to
    for peer in peers:
        pl.semaphore_signal(barrier, inc=1, device_id=peer, device_id_type=MESH)

    def norm_rows(i, start):
        rows = pl.ds(pl.multiple_of(start, 128), 128)
        x = raw[i, rows, :].astype(F32)
        scale = lax.rsqrt(jnp.mean(x * x, axis=-1, keepdims=True) + 1e-05)
        norm[i, rows, :] = (x * scale * gain_buf[...]).astype(BF16)

    def norm_own(t, _):
        norm_rows(0, t * 128)
        return 0

    def norm_halo(m):
        norm_rows(1, m * 128)
        norm_rows(1, HALF + m * 128)

    for copy in w_loads + tok_loads:
        copy.wait()
    pl.semaphore_wait(barrier, len(peers))

    def remote(src, dst, send, recv, to):
        return pltpu.make_async_remote_copy(
            src_ref=src, dst_ref=dst, send_sem=send, recv_sem=recv, device_id=to, device_id_type=MESH
        )

    def lo_copy(j):
        rows = pl.ds(pl.multiple_of(j * CHUNK, CHUNK), CHUNK)
        return remote(raw.at[1 - first, rows, :], raw.at[1, rows, :], lo_send.at[j], lo_recv.at[j], lo_to)

    def hi_copy(j):
        rows = pl.ds(pl.multiple_of(HALF + j * CHUNK, CHUNK), CHUNK)
        return remote(raw.at[1 - last, rows, :], raw.at[1, rows, :], hi_send.at[j], hi_recv.at[j], hi_to)

    def start_lo(j, _):
        lo_copy(j).start()
        return 0

    def start_hi(j, _):
        hi_copy(j).start()
        return 0

    piece = pl.ds(pl.multiple_of(core * HALF + (v * 4 + u) * 32, 32), 32)

    def slab(g, rows):
        if g < 3:
            return wts.at[g + 1, pl.ds(0, 3), rows, :]
        return wts.at[pl.ds(1, 3), 3, rows, :]

    two_sec = jnp.where(core == 0, two_up[0], two_down[0])
    two_seq = jnp.where(core == 0, two_up[1], two_down[1])
    z_to = [down, (two_sec, two_seq), up]
    z_copies = [
        remote(wts.at[0, pl.ds(0, 3), piece, :], wts.at[r + 1, pl.ds(0, 3), piece, :], z_send.at[r], z_recv.at[r], z_to[r])
        for r in range(3)
    ] + [
        remote(wts.at[0, 3, piece, :], wts.at[r + 1, 3, piece, :], z_send.at[3 + r], z_recv.at[3 + r], z_to[r])
        for r in range(3)
    ]
    for copy in z_copies:
        copy.start()

    @pl.when(sec == 0)
    def _():
        lax.fori_loop(0, AHEAD, start_lo, 0)

    @pl.when(sec == 3)
    def _():
        lax.fori_loop(0, AHEAD, start_hi, 0)

    def piece_rows(u1, start=0, size=32):
        return pl.ds(pl.multiple_of(core * HALF + (v * 4 + u1) * 32 + start, 16), size)

    def row_copy(g, d):
        if d < 2:
            rows = piece_rows(u)
        elif d == 2:
            rows = piece_rows((u + 3) % 4, 0, 16)
        else:
            rows = piece_rows((u + 1) % 4, 16, 16)
        return remote(slab(g, rows), slab(g, rows), row_send.at[g * 4 + d], row_recv.at[g * 4 + d], row_to[d % 2])

    def set_rows(v1, start=0, size=128):
        return pl.ds(pl.multiple_of(core * HALF + v1 * 128 + start, 32), size)

    def col_copy(g, d):
        if d < 2:
            rows = set_rows(v)
        elif d == 2:
            rows = set_rows((v + 3) % 4, 0, 64)
        else:
            rows = set_rows((v + 1) % 4, 64, 64)
        return remote(slab(g, rows), slab(g, rows), col_send.at[g * 4 + d], col_recv.at[g * 4 + d], col_to[d % 2])

    def pair_copy(g, d):
        rows = set_rows((v + d) % 4)
        return remote(slab(g, rows), slab(g, rows), pair_send.at[g * 4 + d], pair_recv.at[g * 4 + d], sibling)

    def e1(g):
        if g < 3:
            z_copies[g].wait_recv()
        else:
            for r in range(3):
                z_copies[3 + r].wait_recv()
        for d in range(2):
            row_copy(g, d).start()

    def e2(g):
        for d in range(2):
            row_copy(g, d).wait_recv()
            row_copy(g, 2 + d).start()

    def e3(g):
        for d in range(2):
            row_copy(g, 2 + d).wait_recv()
        for d in range(2):
            col_copy(g, d).start()
        pair_copy(g, 0).start()

    def e4(g):
        col_copy(g, 0).wait_recv()
        col_copy(g, 2).start()
        pair_copy(g, 3).start()
        col_copy(g, 1).wait_recv()
        col_copy(g, 3).start()
        pair_copy(g, 1).start()

    def e5(g):
        col_copy(g, 2).wait_recv()
        col_copy(g, 3).wait_recv()
        pair_copy(g, 2).start()

    def e6(g):
        for d in range(4):
            pair_copy(g, d).wait_recv()

    def halo_step(k):
        @pl.when((sec == 0) & (k + AHEAD < CHUNKS))
        def _():
            lo_copy(k + AHEAD).start()

        @pl.when((sec == 3) & (k + AHEAD < CHUNKS))
        def _():
            hi_copy(k + AHEAD).start()

        j = k - SKEW * (3 - sec)

        @pl.when((j >= 0) & (j < CHUNKS))
        def _():
            lo_copy(j).wait_recv()

            @pl.when(sec != 0)
            def _():
                lo_copy(j).start()

        i = k - SKEW * sec

        @pl.when((i >= 0) & (i < CHUNKS))
        def _():
            hi_copy(i).wait_recv()

            @pl.when(sec != 3)
            def _():
                hi_copy(i).start()

    def own_unit(r, t):
        rows = pl.ds(pl.multiple_of(t * 256, 256), 256)
        x = norm[0, rows, :]
        q = jnp.dot(x, wts[r, 0], preferred_element_type=F32)
        q_buf[r, rows, :] = (q * QSCALE).astype(BF16)
        own_kv[r, 0, rows, :] = jnp.dot(x, wts[r, 1], preferred_element_type=F32).astype(BF16)
        own_kv[r, 1, rows, :] = jnp.dot(x, wts[r, 2], preferred_element_type=F32).astype(BF16)

    def halo_unit(m, r):
        low = pl.ds(pl.multiple_of(m * 128, 128), 128)
        high = pl.ds(pl.multiple_of(HALF + m * 128, 128), 128)
        x = jnp.concatenate([norm[1, low, :], norm[1, high, :]], axis=0)
        for w in range(2):
            y = jnp.dot(x, wts[r, 1 + w], preferred_element_type=F32).astype(BF16)
            halo_kv[w, r, low, :] = y[:128]
            halo_kv[w, r, high, :] = y[128:]

    def own_stores(r):
        return [
            pltpu.make_async_copy(q_buf.at[r], q_out.at[r], store_sem.at[r * 2]),
            pltpu.make_async_copy(own_kv.at[r], kv_out.at[:, r, pl.ds(0, TOK), :], store_sem.at[r * 2 + 1]),
        ]

    def kv_copy(r):
        return remote(own_kv.at[r], kv_out.at[:, r, pl.ds(2 * TOK, TOK), :], kv_send.at[r], kv_recv.at[r], sibling)

    def halo_stores(m):
        copies = []
        for h in range(2):
            copies.append(
                pltpu.make_async_copy(
                    halo_kv.at[:, :, pl.ds(h * HALF + m * 128, 128), :],
                    kv_out.at[:, :, pl.ds(TOK + h * HALF + m * 128, 128), :],
                    hstore_sem.at[m * 2 + h],
                )
            )
        return copies

    def finish_own(r):
        for copy in own_stores(r):
            copy.start()
        kv_copy(r).start()

    def run(first_step, last_step, events, unit):
        def body(k, _):
            halo_step(k)
            for at, event in events:
                pl.when(k == at)(event)
            unit(k)
            return 0

        lax.fori_loop(first_step, last_step + 1, body, 0)

    def seqn(*pairs):
        def go():
            for fn, g in pairs:
                fn(g)

        return go

    gain_load.wait()
    lax.fori_loop(0, TOK // 128, norm_own, 0)

    def unit_r0(k):
        @pl.when(k % 2 == 0)
        def _():
            own_unit(0, k // 2)

    run(0, 7, [(6, seqn((e1, 0), (e1, 1))), (7, seqn((e1, 2), (e1, 3)))], unit_r0)
    finish_own(0)
    run(
        8,
        27,
        [
            (10, seqn((e2, 0), (e2, 1))),
            (11, seqn((e2, 2))),
            (12, seqn((e2, 3))),
            (14, seqn((e3, 0))),
            (15, seqn((e3, 1))),
            (20, seqn((e4, 0), (e3, 2))),
            (23, seqn((e4, 1), (e3, 3))),
            (24, seqn((e5, 0))),
            (25, seqn((norm_halo, 0))),
            (26, lambda: halo_unit(0, 0)),
        ],
        lambda k: None,
    )
    run(28, 32, [(28, seqn((e6, 0), (e4, 2))), (29, seqn((e5, 1))), (32, seqn((e6, 1), (e4, 3), (norm_halo, 1)))], lambda k: pl.when(k < 32)(lambda: own_unit(1, k - 28)))
    finish_own(1)

    def unit_r2(k):
        t = k - 33
        own_unit(2, t)

        @pl.when(t < 3)
        def _():
            halo_unit((t + 1) // 2, (t + 1) % 2)

    run(33, 36, [(34, seqn((e5, 2)))], unit_r2)
    finish_own(2)
    run(37, 40, [(37, seqn((e6, 2))), (38, seqn((e5, 3)))], lambda k: own_unit(3, k - 37))
    finish_own(3)

    def unit_halo(k):
        t = k - 41
        halo_unit(jnp.where(t < 4, t % 2, 2), jnp.where(t < 4, 2 + t // 2, t - 4))

    run(41, STEPS - 1, [(42, seqn((norm_halo, 2))), (44, seqn((e6, 3)))], unit_halo)
    halo_unit(2, 2)
    halo_unit(2, 3)
    norm_halo(3)
    wo_store = pltpu.make_async_copy(wts.at[:, 3], wo_out, wload_sem.at[7])
    wo_store.start()
    for m in range(3):
        for copy in halo_stores(m):
            copy.start()

    def tail(r, _):
        halo_unit(3, r)
        return 0

    lax.fori_loop(0, GROUP, tail, 0)
    for copy in halo_stores(3):
        copy.start()

    def drain(j, _):
        lo_copy(j).wait_send()
        hi_copy(j).wait_send()
        return 0

    lax.fori_loop(0, CHUNKS, drain, 0)
    for copy in z_copies:
        copy.wait_send()
    for g in range(4):
        for d in range(4):
            row_copy(g, d).wait_send()
            col_copy(g, d).wait_send()
            pair_copy(g, d).wait_send()
    for r in range(GROUP):
        for copy in own_stores(r):
            copy.wait()
        kv_copy(r).wait()
    wo_store.wait()
    for m in range(4):
        for copy in halo_stores(m):
            copy.wait()


def project(tokens, gain, wq, wk, wv, wo):
    any_spec = pl.BlockSpec(memory_space=pltpu.HBM)
    dma = pltpu.SemaphoreType.DMA
    return pl.pallas_call(
        gather_project,
        out_shape=[
            jax.ShapeDtypeStruct((GROUP, TOK, COLS), BF16),
            jax.ShapeDtypeStruct((2, GROUP, 3 * TOK, COLS), BF16),
            jax.ShapeDtypeStruct((GROUP, WIDTH, COLS), BF16),
        ],
        in_specs=[any_spec] * 6,
        out_specs=[any_spec] * 3,
        scratch_shapes=[
            pltpu.VMEM((1, WIDTH), F32),
            pltpu.VMEM((2, TOK, WIDTH), BF16),
            pltpu.VMEM((2, TOK, WIDTH), BF16),
            pltpu.VMEM((GROUP, 4, WIDTH, COLS), BF16),
            pltpu.VMEM((GROUP, TOK, COLS), BF16),
            pltpu.VMEM((GROUP, 2, TOK, COLS), BF16),
            pltpu.VMEM((2, GROUP, TOK, COLS), BF16),
            dma, dma((4,)), dma((8,)),
            dma((CHUNKS,)), dma((CHUNKS,)), dma((CHUNKS,)), dma((CHUNKS,)),
            dma((6,)), dma((6,)), dma((16,)), dma((16,)), dma((16,)), dma((16,)), dma((16,)), dma((16,)),
            dma((4,)), dma((4,)), dma((8,)), dma((8,)),
        ],
        compiler_params=pltpu.CompilerParams(
            collective_id=0, has_side_effects=True, vmem_limit_bytes=62 * 2**20
        ),
        name="gather_project",
    )(tokens, gain, wq, wk, wv, wo)


PAIRS = 4


def attend_decode(
    near_ref, counts_ref, stain_ref,
    q_ref, k_ref, v_ref, wo_ref, tok_ref, gain_ref, sw_ref,
    out_ref, att, e_scr,
):
    step = pl.program_id(0)
    seq = lax.axis_index("seq")
    blocks = TOK // BLOCK

    def place(near):
        owner = near // blocks - seq
        part = jnp.where(owner == 0, 0, jnp.where(owner == 2 * (seq % 2) - 1, 1, 2))
        return pl.multiple_of((part * blocks + near % blocks) * BLOCK, BLOCK)

    lane = lax.broadcasted_iota(jnp.int32, (BLOCK, BLOCK), 1)

    def block(i, _):
        rows = pl.ds(pl.multiple_of(i * BLOCK, BLOCK), BLOCK)
        starts = [place(near_ref[i, j]) for j in range(NEIGH)]

        def run(n):
            for p in range(PAIRS):
                r, c = p // 2, (p % 2) * BLOCK
                q = q_ref[r, rows, c : c + BLOCK]
                zero = jnp.zeros_like(q)
                both = jnp.concatenate([jnp.where(lane < HEAD_DIM, q, zero), jnp.where(lane < HEAD_DIM, zero, q)], axis=0)
                k = jnp.concatenate([k_ref[0, r, pl.ds(starts[j], BLOCK), c : c + BLOCK] for j in range(n)], axis=0)
                s = lax.dot_general(both, k, (((1,), (1,)), ((), ())), preferred_element_type=F32)
                top = jnp.max(s, axis=1, keepdims=True)
                e_scr[p, :, : n * BLOCK] = jnp.exp2(s - top).astype(BF16)
            for p in range(PAIRS):
                r, c = p // 2, (p % 2) * BLOCK
                v = jnp.concatenate([v_ref[0, r, pl.ds(starts[j], BLOCK), c : c + BLOCK] for j in range(n)], axis=0)
                v = jnp.concatenate([v, jnp.ones((n * BLOCK, BLOCK), BF16)], axis=1)
                o = jnp.dot(e_scr[p, :, : n * BLOCK], v, preferred_element_type=F32)
                o = o[:, :BLOCK] / o[:, BLOCK:]
                att[step * 2 + r, rows, c : c + BLOCK] = jnp.where(lane < HEAD_DIM, o[:BLOCK], o[BLOCK:]).astype(BF16)

        for n in range(3, NEIGH + 1):
            pl.when(counts_ref[i] == n)(functools.partial(run, n))
        return 0

    lax.fori_loop(0, TOK // BLOCK, block, 0)

    @pl.when(step == GROUP // 2 - 1)
    def _():
        gain = gain_ref[pl.ds(stain_ref[0], 1), :]

        def rows_out(t, _):
            rows = pl.ds(pl.multiple_of(t * 256, 256), 256)
            x = jnp.concatenate([att[r, rows, :] for r in range(GROUP)], axis=1)
            parts = []
            for c in range(GROUP):
                w = jnp.concatenate([wo_ref[r, c * COLS : (c + 1) * COLS, :] for r in range(GROUP)], axis=0)
                parts.append(jnp.dot(x, w, preferred_element_type=F32))
            mixed = jnp.concatenate(parts, axis=1)
            encoded = (tok_ref[rows, :].astype(F32) + mixed).astype(BF16).astype(F32)
            scale = lax.rsqrt(jnp.mean(encoded * encoded, axis=-1, keepdims=True) + 1e-05)
            decoded = (encoded * scale * gain).astype(BF16)
            out_ref[0, rows, :] = jnp.dot(decoded, sw_ref[0], preferred_element_type=F32).astype(BF16)
            return 0

        lax.fori_loop(0, 4, rows_out, 0)


def attention(neighbours, counts, stain, q, kv, wo, tokens, stain_gain, stain_weight):
    half = GROUP // 2
    return pl.pallas_call(
        attend_decode,
        out_shape=jax.ShapeDtypeStruct((1, TOK, PIX), BF16),
        grid_spec=pltpu.PrefetchScalarGridSpec(
            num_scalar_prefetch=3,
            grid=(2,),
            in_specs=[
                pl.BlockSpec((half, TOK, COLS), lambda g, *_: (g, 0, 0)),
                pl.BlockSpec((1, half, 3 * TOK, COLS), lambda g, *_: (0, g, 0, 0)),
                pl.BlockSpec((1, half, 3 * TOK, COLS), lambda g, *_: (1, g, 0, 0)),
                pl.BlockSpec((GROUP, WIDTH, COLS), lambda g, *_: (0, 0, 0), pipeline_mode=pl.Buffered(1)),
                pl.BlockSpec((TOK, WIDTH), lambda g, *_: (0, 0), pipeline_mode=pl.Buffered(1)),
                pl.BlockSpec(memory_space=pltpu.VMEM),
                pl.BlockSpec((1, WIDTH, PIX), lambda g, near, counts, stain: (stain[0], 0, 0), pipeline_mode=pl.Buffered(1)),
            ],
            out_specs=pl.BlockSpec((1, TOK, PIX), lambda g, *_: (0, 0, 0)),
            scratch_shapes=[
                pltpu.VMEM((GROUP, TOK, COLS), BF16),
                pltpu.VMEM((PAIRS, 2 * BLOCK, NEIGH * BLOCK), BF16),
            ],
        ),
        compiler_params=pltpu.CompilerParams(vmem_limit_bytes=56 * 2**20),
        name="attend_decode",
    )(neighbours, counts, stain, q, kv, kv, wo, tokens, stain_gain, stain_weight)


def per_device(
    tokens, enc_gain, w_query, w_key, w_value, w_out, neighbours, counts, stain_of_section, stain_gain, stain_weight
):
    q, kv, wo = project(tokens, enc_gain[None, :], w_query, w_key, w_value, w_out)
    return attention(neighbours, counts, stain_of_section, q, kv, wo, tokens, stain_gain, stain_weight)


def solution(mesh):
    placed = (
        P("seq", None),
        P(),
        P(None, "section"),
        P(None, "section"),
        P(None, "section"),
        P("section", None),
        P("seq", None),
        P("seq"),
        P("section"),
        P(),
        P(),
    )
    return jax.shard_map(
        per_device, mesh=mesh, in_specs=placed, out_specs=P("section", "seq", None), check_vma=False
    )
```

```python
import functools

import jax
import jax.numpy as jnp
from jax import lax
from jax.experimental import pallas as pl
from jax.experimental.pallas import tpu as pltpu
from jax.sharding import PartitionSpec as P

HEAD_DIM = 64
BLOCK = 128
NEIGH = 8
TOK = 1024
WIDTH = 1024
PIX = 768
GROUP = 4
COLS = WIDTH // GROUP
CHUNK = 16
HALF = TOK // 2
CHUNKS = HALF // CHUNK
SKEW = 5
AHEAD = 6
STEPS = CHUNKS + SKEW * (GROUP - 1)
QSCALE = 0.125 * 1.4426950408889634

F32 = jnp.float32
BF16 = jnp.bfloat16
MESH = pl.DeviceIdType.MESH


def gather_project(
    tok_hbm, gain_hbm, wq_hbm, wk_hbm, wv_hbm, wo_hbm,
    q_out, kv_out, wo_out,
    gain_buf, raw, norm, wts, q_buf, own_kv, halo_kv,
    gain_sem, tok_sem, wload_sem, lo_send, lo_recv, hi_send, hi_recv,
    z_send, z_recv, row_send, row_recv, col_send, col_recv, pair_send, pair_recv,
    kv_send, kv_recv, store_sem, hstore_sem,
):
    sec = lax.axis_index("section")
    seq = lax.axis_index("seq")
    core = seq % 2
    zhi = (seq // 2) % 2
    yy = (seq // 4) % 4
    xx = seq // 16
    u = xx * (1 - core) + yy * core
    v = yy * (1 - core) + xx * core

    def seq_at(u1, v1):
        x1 = u1 * (1 - core) + v1 * core
        y1 = v1 * (1 - core) + u1 * core
        return ((x1 * 4 + y1) * 2 + zhi) * 2 + core

    def z_at(step):
        z1 = (zhi * 4 + sec + step + 8) % 8
        return (z1 % 4, seq + (z1 // 4 - zhi) * 2)

    sibling = (sec, seq + 1 - 2 * core)
    partner = (seq + 2 * core - 1 + 64) % 64
    up, down = z_at(1), z_at(7)
    two_up, two_down = z_at(2), z_at(6)
    first = jnp.where(sec == 0, 1, 0)
    last = jnp.where(sec == 3, 1, 0)
    lo_to = ((sec + 3) % 4, jnp.where(sec == 0, partner, seq))
    hi_to = ((sec + 1) % 4, jnp.where(sec == 3, partner, seq))
    row_to = [(sec, seq_at((u + d) % 4, v)) for d in (1, 3)]
    col_to = [(sec, seq_at(u, (v + d) % 4)) for d in (1, 3)]

    tok_loads = []
    for i in range(4):
        rows = pl.ds(i * 256, 256)
        tok_loads.append(pltpu.make_async_copy(tok_hbm.at[rows, :], raw.at[0, rows, :], tok_sem.at[i]))
    w_loads = [
        pltpu.make_async_copy(src, wts.at[0, i], wload_sem.at[i])
        for i, src in enumerate((wq_hbm, wk_hbm, wv_hbm))
    ]
    for i in range(4):
        w_loads.append(
            pltpu.make_async_copy(
                wo_hbm.at[:, pl.ds(i * COLS, COLS)],
                wts.at[0, 3, pl.ds(i * COLS, COLS), :],
                wload_sem.at[3 + i],
            )
        )
    gain_load = pltpu.make_async_copy(gain_hbm, gain_buf, gain_sem)
    for copy in [gain_load] + tok_loads + w_loads:
        copy.start()

    barrier = pltpu.get_barrier_semaphore()
    peers = [sibling, up, down, two_up, two_down, lo_to, hi_to] + row_to + col_to
    for peer in peers:
        pl.semaphore_signal(barrier, inc=1, device_id=peer, device_id_type=MESH)

    def norm_rows(i, start):
        rows = pl.ds(pl.multiple_of(start, 128), 128)
        x = raw[i, rows, :].astype(F32)
        scale = lax.rsqrt(jnp.mean(x * x, axis=-1, keepdims=True) + 1e-05)
        norm[i, rows, :] = (x * scale * gain_buf[...]).astype(BF16)

    def norm_own(t, _):
        norm_rows(0, t * 128)
        return 0

    def norm_halo(m):
        norm_rows(1, m * 128)
        norm_rows(1, HALF + m * 128)

    for copy in w_loads + tok_loads:
        copy.wait()
    pl.semaphore_wait(barrier, len(peers))

    def remote(src, dst, send, recv, to):
        return pltpu.make_async_remote_copy(
            src_ref=src, dst_ref=dst, send_sem=send, recv_sem=recv, device_id=to, device_id_type=MESH
        )

    def lo_copy(j):
        rows = pl.ds(pl.multiple_of(j * CHUNK, CHUNK), CHUNK)
        return remote(raw.at[1 - first, rows, :], raw.at[1, rows, :], lo_send.at[j], lo_recv.at[j], lo_to)

    def hi_copy(j):
        rows = pl.ds(pl.multiple_of(HALF + j * CHUNK, CHUNK), CHUNK)
        return remote(raw.at[1 - last, rows, :], raw.at[1, rows, :], hi_send.at[j], hi_recv.at[j], hi_to)

    def start_lo(j, _):
        lo_copy(j).start()
        return 0

    def start_hi(j, _):
        hi_copy(j).start()
        return 0

    piece = pl.ds(pl.multiple_of(core * HALF + (v * 4 + u) * 32, 32), 32)

    def slab(g, rows):
        if g < 3:
            return wts.at[g + 1, pl.ds(0, 3), rows, :]
        return wts.at[pl.ds(1, 3), 3, rows, :]

    two_sec = jnp.where(core == 0, two_up[0], two_down[0])
    two_seq = jnp.where(core == 0, two_up[1], two_down[1])
    z_to = [down, (two_sec, two_seq), up]
    z_copies = [
        remote(wts.at[0, pl.ds(0, 3), piece, :], wts.at[r + 1, pl.ds(0, 3), piece, :], z_send.at[r], z_recv.at[r], z_to[r])
        for r in range(3)
    ] + [
        remote(wts.at[0, 3, piece, :], wts.at[r + 1, 3, piece, :], z_send.at[3 + r], z_recv.at[3 + r], z_to[r])
        for r in range(3)
    ]
    for copy in z_copies:
        copy.start()

    @pl.when(sec == 0)
    def _():
        lax.fori_loop(0, AHEAD, start_lo, 0)

    @pl.when(sec == 3)
    def _():
        lax.fori_loop(0, AHEAD, start_hi, 0)

    def piece_rows(u1, start=0, size=32):
        return pl.ds(pl.multiple_of(core * HALF + (v * 4 + u1) * 32 + start, 16), size)

    def row_copy(g, d):
        if d < 2:
            rows = piece_rows(u)
        elif d == 2:
            rows = piece_rows((u + 3) % 4, 0, 16)
        else:
            rows = piece_rows((u + 1) % 4, 16, 16)
        return remote(slab(g, rows), slab(g, rows), row_send.at[g * 4 + d], row_recv.at[g * 4 + d], row_to[d % 2])

    def set_rows(v1, start=0, size=128):
        return pl.ds(pl.multiple_of(core * HALF + v1 * 128 + start, 32), size)

    def col_copy(g, d):
        if d < 2:
            rows = set_rows(v)
        elif d == 2:
            rows = set_rows((v + 3) % 4, 0, 64)
        else:
            rows = set_rows((v + 1) % 4, 64, 64)
        return remote(slab(g, rows), slab(g, rows), col_send.at[g * 4 + d], col_recv.at[g * 4 + d], col_to[d % 2])

    def pair_copy(g, d):
        rows = set_rows((v + d) % 4)
        return remote(slab(g, rows), slab(g, rows), pair_send.at[g * 4 + d], pair_recv.at[g * 4 + d], sibling)

    def e1(g):
        if g < 3:
            z_copies[g].wait_recv()
        else:
            for r in range(3):
                z_copies[3 + r].wait_recv()
        for d in range(2):
            row_copy(g, d).start()

    def e2(g):
        for d in range(2):
            row_copy(g, d).wait_recv()
            row_copy(g, 2 + d).start()

    def e3(g):
        for d in range(2):
            row_copy(g, 2 + d).wait_recv()
        for d in range(2):
            col_copy(g, d).start()
        pair_copy(g, 0).start()

    def e4(g):
        col_copy(g, 0).wait_recv()
        col_copy(g, 2).start()
        pair_copy(g, 3).start()
        col_copy(g, 1).wait_recv()
        col_copy(g, 3).start()
        pair_copy(g, 1).start()

    def e5(g):
        col_copy(g, 2).wait_recv()
        col_copy(g, 3).wait_recv()
        pair_copy(g, 2).start()

    def e6(g):
        for d in range(4):
            pair_copy(g, d).wait_recv()

    def halo_step(k):
        @pl.when((sec == 0) & (k + AHEAD < CHUNKS))
        def _():
            lo_copy(k + AHEAD).start()

        @pl.when((sec == 3) & (k + AHEAD < CHUNKS))
        def _():
            hi_copy(k + AHEAD).start()

        j = k - SKEW * (3 - sec)

        @pl.when((j >= 0) & (j < CHUNKS))
        def _():
            lo_copy(j).wait_recv()

            @pl.when(sec != 0)
            def _():
                lo_copy(j).start()

        i = k - SKEW * sec

        @pl.when((i >= 0) & (i < CHUNKS))
        def _():
            hi_copy(i).wait_recv()

            @pl.when(sec != 3)
            def _():
                hi_copy(i).start()

    def own_unit(r, t):
        rows = pl.ds(pl.multiple_of(t * 512, 512), 512)
        x = norm[0, rows, :]
        q = jnp.dot(x, wts[r, 0], preferred_element_type=F32)
        q_buf[r, rows, :] = (q * QSCALE).astype(BF16)
        own_kv[r, 0, rows, :] = jnp.dot(x, wts[r, 1], preferred_element_type=F32).astype(BF16)
        own_kv[r, 1, rows, :] = jnp.dot(x, wts[r, 2], preferred_element_type=F32).astype(BF16)

    def halo_unit(m, count, r):
        size = 128 * count
        low = pl.ds(m * 128, size)
        high = pl.ds(HALF + m * 128, size)
        x = jnp.concatenate([norm[1, low, :], norm[1, high, :]], axis=0)
        for w in range(2):
            y = jnp.dot(x, wts[r, 1 + w], preferred_element_type=F32).astype(BF16)
            halo_kv[w, r, low, :] = y[:size]
            halo_kv[w, r, high, :] = y[size:]

    def halo_all(m):
        for r in range(GROUP):
            halo_unit(m, 1, r)

    def own_stores(r):
        return [
            pltpu.make_async_copy(q_buf.at[r], q_out.at[r], store_sem.at[r * 2]),
            pltpu.make_async_copy(own_kv.at[r], kv_out.at[:, r, pl.ds(0, TOK), :], store_sem.at[r * 2 + 1]),
        ]

    def kv_copy(r):
        return remote(own_kv.at[r], kv_out.at[:, r, pl.ds(2 * TOK, TOK), :], kv_send.at[r], kv_recv.at[r], sibling)

    def halo_stores(m):
        copies = []
        for h in range(2):
            copies.append(
                pltpu.make_async_copy(
                    halo_kv.at[:, :, pl.ds(h * HALF + m * 128, 128), :],
                    kv_out.at[:, :, pl.ds(TOK + h * HALF + m * 128, 128), :],
                    hstore_sem.at[m * 2 + h],
                )
            )
        return copies

    def finish_own(r):
        for copy in own_stores(r):
            copy.start()
        kv_copy(r).start()

    def run(first_step, last_step, events, unit):
        def body(k, _):
            halo_step(k)
            for at, event in events:
                pl.when(k == at)(event)
            unit(k)
            return 0

        lax.fori_loop(first_step, last_step + 1, body, 0)

    def seqn(*pairs):
        def go():
            for fn, g in pairs:
                fn(g)

        return go

    gain_load.wait()
    lax.fori_loop(0, TOK // 128, norm_own, 0)

    def unit_r0(k):
        @pl.when(k % 4 == 0)
        def _():
            own_unit(0, k // 4)

    run(0, 7, [(6, seqn((e1, 0), (e1, 1))), (7, seqn((e1, 2), (e1, 3)))], unit_r0)
    finish_own(0)
    run(
        8,
        27,
        [
            (10, seqn((e2, 0), (e2, 1))),
            (11, seqn((e2, 2))),
            (12, seqn((e2, 3))),
            (14, seqn((e3, 0))),
            (15, seqn((e3, 1))),
            (20, seqn((e4, 0), (e3, 2))),
            (23, seqn((e4, 1), (e3, 3))),
            (24, seqn((e5, 0))),
            (25, seqn((norm_halo, 0))),
        ],
        lambda k: None,
    )
    run(28, 32, [(28, seqn((e6, 0), (e4, 2))), (29, seqn((e5, 1))), (32, seqn((e6, 1), (e4, 3), (norm_halo, 1)))], lambda k: pl.when((k == 28) | (k == 30))(lambda: own_unit(1, (k - 28) // 2)))
    finish_own(1)

    def unit_r2(k):
        t = k - 33

        @pl.when(t % 2 == 0)
        def _():
            own_unit(2, t // 2)
            halo_unit(0, 2, t // 2)

    run(33, 36, [(34, seqn((e5, 2)))], unit_r2)
    finish_own(2)

    def unit_r3(k):
        t = k - 37

        @pl.when(t % 2 == 0)
        def _():
            own_unit(3, t // 2)
            halo_unit(0, 2, 2 + t // 2)

    run(37, 40, [(37, seqn((e6, 2))), (38, seqn((e5, 3)))], unit_r3)
    finish_own(3)
    run(
        41,
        STEPS - 1,
        [(42, seqn((norm_halo, 2))), (43, seqn((e6, 3)))],
        lambda k: pl.when(k == 43)(lambda: halo_all(2)),
    )
    norm_halo(3)
    wo_store = pltpu.make_async_copy(wts.at[:, 3], wo_out, wload_sem.at[7])
    wo_store.start()
    for m in range(3):
        for copy in halo_stores(m):
            copy.start()

    halo_all(3)
    for copy in halo_stores(3):
        copy.start()

    def drain(j, _):
        lo_copy(j).wait_send()
        hi_copy(j).wait_send()
        return 0

    lax.fori_loop(0, CHUNKS, drain, 0)
    for copy in z_copies:
        copy.wait_send()
    for g in range(4):
        for d in range(4):
            row_copy(g, d).wait_send()
            col_copy(g, d).wait_send()
            pair_copy(g, d).wait_send()
    for r in range(GROUP):
        for copy in own_stores(r):
            copy.wait()
        kv_copy(r).wait()
    wo_store.wait()
    for m in range(4):
        for copy in halo_stores(m):
            copy.wait()


def project(tokens, gain, wq, wk, wv, wo):
    any_spec = pl.BlockSpec(memory_space=pltpu.HBM)
    dma = pltpu.SemaphoreType.DMA
    return pl.pallas_call(
        gather_project,
        out_shape=[
            jax.ShapeDtypeStruct((GROUP, TOK, COLS), BF16),
            jax.ShapeDtypeStruct((2, GROUP, 3 * TOK, COLS), BF16),
            jax.ShapeDtypeStruct((GROUP, WIDTH, COLS), BF16),
        ],
        in_specs=[any_spec] * 6,
        out_specs=[any_spec] * 3,
        scratch_shapes=[
            pltpu.VMEM((1, WIDTH), F32),
            pltpu.VMEM((2, TOK, WIDTH), BF16),
            pltpu.VMEM((2, TOK, WIDTH), BF16),
            pltpu.VMEM((GROUP, 4, WIDTH, COLS), BF16),
            pltpu.VMEM((GROUP, TOK, COLS), BF16),
            pltpu.VMEM((GROUP, 2, TOK, COLS), BF16),
            pltpu.VMEM((2, GROUP, TOK, COLS), BF16),
            dma, dma((4,)), dma((8,)),
            dma((CHUNKS,)), dma((CHUNKS,)), dma((CHUNKS,)), dma((CHUNKS,)),
            dma((6,)), dma((6,)), dma((16,)), dma((16,)), dma((16,)), dma((16,)), dma((16,)), dma((16,)),
            dma((4,)), dma((4,)), dma((8,)), dma((8,)),
        ],
        compiler_params=pltpu.CompilerParams(
            collective_id=0, has_side_effects=True, vmem_limit_bytes=62 * 2**20
        ),
        name="gather_project",
    )(tokens, gain, wq, wk, wv, wo)


PAIRS = 4
LAG = 4
ROWS = 512


def attend_decode(
    near_ref, counts_ref, stain_ref, q_hbm, kv_hbm, wo_hbm, tok_hbm, gain_ref, sw_hbm,
    out_hbm,
    q_buf, k_buf, v_buf, wo_buf, tok_buf, sw_buf, att, e_scr, out_buf,
    q_sem, k_sem, v_sem, late_sem, out_sem,
):
    seq = lax.axis_index("seq")
    blocks = TOK // BLOCK
    stain = stain_ref[0]

    def loads(r):
        return [
            pltpu.make_async_copy(q_hbm.at[r], q_buf.at[r], q_sem.at[r]),
            pltpu.make_async_copy(kv_hbm.at[0, r], k_buf.at[r], k_sem.at[r]),
            pltpu.make_async_copy(kv_hbm.at[1, r], v_buf.at[r], v_sem.at[r]),
        ]

    late = [
        pltpu.make_async_copy(wo_hbm, wo_buf, late_sem.at[0]),
        pltpu.make_async_copy(tok_hbm, tok_buf, late_sem.at[1]),
        pltpu.make_async_copy(sw_hbm.at[stain], sw_buf, late_sem.at[2]),
    ]
    for r in range(GROUP):
        for copy in loads(r):
            copy.start()
    for copy in late:
        copy.start()

    def place(near):
        owner = near // blocks - seq
        part = jnp.where(owner == 0, 0, jnp.where(owner == 2 * (seq % 2) - 1, 1, 2))
        return pl.multiple_of((part * blocks + near % blocks) * BLOCK, BLOCK)

    lane = lax.broadcasted_iota(jnp.int32, (BLOCK, BLOCK), 1)

    def block(i, h):
        rows = pl.ds(pl.multiple_of(i * BLOCK, BLOCK), BLOCK)
        starts = [place(near_ref[i, j]) for j in range(NEIGH)]

        def score(p, n):
            r, c = 2 * h + p // 2, (p % 2) * BLOCK
            q = q_buf[r, rows, c : c + BLOCK]
            zero = jnp.zeros_like(q)
            both = jnp.concatenate([jnp.where(lane < HEAD_DIM, q, zero), jnp.where(lane < HEAD_DIM, zero, q)], axis=0)
            k = jnp.concatenate([k_buf[r, pl.ds(starts[j], BLOCK), c : c + BLOCK] for j in range(n)], axis=0)
            s = lax.dot_general(both, k, (((1,), (1,)), ((), ())), preferred_element_type=F32)
            top = jnp.max(s, axis=1, keepdims=True)
            e_scr[p, :, : n * BLOCK] = jnp.exp2(s - top).astype(BF16)

        def mix(p, n):
            r, c = 2 * h + p // 2, (p % 2) * BLOCK
            v = jnp.concatenate([v_buf[r, pl.ds(starts[j], BLOCK), c : c + BLOCK] for j in range(n)], axis=0)
            v = jnp.concatenate([v, jnp.ones((n * BLOCK, BLOCK), BF16)], axis=1)
            o = jnp.dot(e_scr[p, :, : n * BLOCK], v, preferred_element_type=F32)
            o = o[:, :BLOCK] / o[:, BLOCK:]
            att[r, rows, c : c + BLOCK] = jnp.where(lane < HEAD_DIM, o[:BLOCK], o[BLOCK:]).astype(BF16)

        def run(n):
            for t in range(PAIRS + LAG):
                if t < PAIRS:
                    score(t, n)
                if t >= LAG:
                    mix(t - LAG, n)

        for n in range(3, NEIGH + 1):
            pl.when(counts_ref[i] == n)(functools.partial(run, n))

    def half(h, _):
        for r in range(2):
            for copy in loads(2 * h + r):
                copy.wait()

        def one(i, _):
            block(i, h)
            return 0

        lax.fori_loop(0, blocks, one, 0)
        return 0

    lax.fori_loop(0, GROUP // 2, half, 0)

    for copy in late:
        copy.wait()
    gain = gain_ref[pl.ds(stain, 1), :]

    def store(t):
        rows = pl.ds(t * ROWS, ROWS)
        return pltpu.make_async_copy(out_buf.at[rows, :], out_hbm.at[0, rows, :], out_sem.at[t])

    def rows_out(t, _):
        rows = pl.ds(pl.multiple_of(t * ROWS, ROWS), ROWS)
        x = jnp.concatenate([att[r, rows, :] for r in range(GROUP)], axis=1)
        parts = []
        for c in range(GROUP):
            w = jnp.concatenate([wo_buf[r, c * COLS : (c + 1) * COLS, :] for r in range(GROUP)], axis=0)
            parts.append(jnp.dot(x, w, preferred_element_type=F32))
        mixed = jnp.concatenate(parts, axis=1)
        encoded = (tok_buf[rows, :].astype(F32) + mixed).astype(BF16).astype(F32)
        scale = lax.rsqrt(jnp.mean(encoded * encoded, axis=-1, keepdims=True) + 1e-05)
        decoded = (encoded * scale * gain).astype(BF16)
        out_buf[rows, :] = jnp.dot(decoded, sw_buf[...], preferred_element_type=F32).astype(BF16)
        store(t).start()
        return 0

    lax.fori_loop(0, TOK // ROWS, rows_out, 0)
    for t in range(TOK // ROWS):
        store(t).wait()


def attention(neighbours, counts, stain, q, kv, wo, tokens, stain_gain, stain_weight):
    hbm = pl.BlockSpec(memory_space=pltpu.HBM)
    smem = pl.BlockSpec(memory_space=pltpu.SMEM)
    dma = pltpu.SemaphoreType.DMA
    return pl.pallas_call(
        attend_decode,
        out_shape=jax.ShapeDtypeStruct((1, TOK, PIX), BF16),
        in_specs=[smem] * 3 + [hbm] * 4 + [pl.BlockSpec(memory_space=pltpu.VMEM), hbm],
        out_specs=hbm,
        scratch_shapes=[
            pltpu.VMEM((GROUP, TOK, COLS), BF16),
            pltpu.VMEM((GROUP, 3 * TOK, COLS), BF16),
            pltpu.VMEM((GROUP, 3 * TOK, COLS), BF16),
            pltpu.VMEM((GROUP, WIDTH, COLS), BF16),
            pltpu.VMEM((TOK, WIDTH), BF16),
            pltpu.VMEM((WIDTH, PIX), BF16),
            pltpu.VMEM((GROUP, TOK, COLS), BF16),
            pltpu.VMEM((PAIRS, 2 * BLOCK, NEIGH * BLOCK), BF16),
            pltpu.VMEM((TOK, PIX), BF16),
            dma((GROUP,)), dma((GROUP,)), dma((GROUP,)), dma((3,)), dma((TOK // ROWS,)),
        ],
        compiler_params=pltpu.CompilerParams(vmem_limit_bytes=62 * 2**20),
        name="attend_decode",
    )(neighbours, counts, stain, q, kv, wo, tokens, stain_gain, stain_weight)


def per_device(
    tokens, enc_gain, w_query, w_key, w_value, w_out, neighbours, counts, stain_of_section, stain_gain, stain_weight
):
    q, kv, wo = project(tokens, enc_gain[None, :], w_query, w_key, w_value, w_out)
    return attention(neighbours, counts, stain_of_section, q, kv, wo, tokens, stain_gain, stain_weight)


def solution(mesh):
    placed = (
        P("seq", None),
        P(),
        P(None, "section"),
        P(None, "section"),
        P(None, "section"),
        P("section", None),
        P("seq", None),
        P("seq"),
        P("section"),
        P(),
        P(),
    )
    return jax.shard_map(
        per_device, mesh=mesh, in_specs=placed, out_specs=P("section", "seq", None), check_vma=False
    )
```

```python
import functools

import jax
import jax.numpy as jnp
from jax import lax
from jax.experimental import pallas as pl
from jax.experimental.pallas import tpu as pltpu
from jax.sharding import PartitionSpec as P

HEAD_DIM = 64
BLOCK = 128
NEIGH = 8
TOK = 1024
WIDTH = 1024
PIX = 768
GROUP = 4
COLS = WIDTH // GROUP
CHUNK = 16
HALF = TOK // 2
CHUNKS = HALF // CHUNK
SKEW = 5
AHEAD = 6
STEPS = CHUNKS + SKEW * (GROUP - 1)
QSCALE = 0.125 * 1.4426950408889634

F32 = jnp.float32
BF16 = jnp.bfloat16
MESH = pl.DeviceIdType.MESH


def gather_project(
    tok_hbm, gain_hbm, wq_hbm, wk_hbm, wv_hbm, wo_hbm,
    q_out, kv_out, wo_out,
    gain_buf, raw, norm, wts, q_buf, own_kv, halo_kv,
    gain_sem, tok_sem, wload_sem, lo_send, lo_recv, hi_send, hi_recv,
    z_send, z_recv, row_send, row_recv, col_send, col_recv, pair_send, pair_recv,
    kv_send, kv_recv, store_sem, hstore_sem,
):
    sec = lax.axis_index("section")
    seq = lax.axis_index("seq")
    core = seq % 2
    zhi = (seq // 2) % 2
    yy = (seq // 4) % 4
    xx = seq // 16
    u = xx * (1 - core) + yy * core
    v = yy * (1 - core) + xx * core

    def seq_at(u1, v1):
        x1 = u1 * (1 - core) + v1 * core
        y1 = v1 * (1 - core) + u1 * core
        return ((x1 * 4 + y1) * 2 + zhi) * 2 + core

    def z_at(step):
        z1 = (zhi * 4 + sec + step + 8) % 8
        return (z1 % 4, seq + (z1 // 4 - zhi) * 2)

    sibling = (sec, seq + 1 - 2 * core)
    partner = (seq + 2 * core - 1 + 64) % 64
    up, down = z_at(1), z_at(7)
    two_up, two_down = z_at(2), z_at(6)
    first = jnp.where(sec == 0, 1, 0)
    last = jnp.where(sec == 3, 1, 0)
    lo_to = ((sec + 3) % 4, jnp.where(sec == 0, partner, seq))
    hi_to = ((sec + 1) % 4, jnp.where(sec == 3, partner, seq))
    row_to = [(sec, seq_at((u + d) % 4, v)) for d in (1, 3)]
    col_to = [(sec, seq_at(u, (v + d) % 4)) for d in (1, 3)]

    tok_loads = []
    for i in range(4):
        rows = pl.ds(i * 256, 256)
        tok_loads.append(pltpu.make_async_copy(tok_hbm.at[rows, :], raw.at[0, rows, :], tok_sem.at[i]))
    w_loads = [
        pltpu.make_async_copy(src, wts.at[0, i], wload_sem.at[i])
        for i, src in enumerate((wq_hbm, wk_hbm, wv_hbm))
    ]
    for i in range(4):
        w_loads.append(
            pltpu.make_async_copy(
                wo_hbm.at[:, pl.ds(i * COLS, COLS)],
                wts.at[0, 3, pl.ds(i * COLS, COLS), :],
                wload_sem.at[3 + i],
            )
        )
    gain_load = pltpu.make_async_copy(gain_hbm, gain_buf, gain_sem)
    for copy in w_loads + tok_loads + [gain_load]:
        copy.start()

    barrier = pltpu.get_barrier_semaphore()
    peers = [sibling, up, down, two_up, two_down, lo_to, hi_to] + row_to + col_to
    for peer in peers:
        pl.semaphore_signal(barrier, inc=1, device_id=peer, device_id_type=MESH)

    def norm_rows(i, start):
        rows = pl.ds(pl.multiple_of(start, 128), 128)
        x = raw[i, rows, :].astype(F32)
        scale = lax.rsqrt(jnp.mean(x * x, axis=-1, keepdims=True) + 1e-05)
        norm[i, rows, :] = (x * scale * gain_buf[...]).astype(BF16)

    def norm_own(t, _):
        norm_rows(0, t * 128)
        return 0

    def norm_halo(m):
        norm_rows(1, m * 128)
        norm_rows(1, HALF + m * 128)

    for copy in w_loads:
        copy.wait()
    pl.semaphore_wait(barrier, len(peers))

    def remote(src, dst, send, recv, to):
        return pltpu.make_async_remote_copy(
            src_ref=src, dst_ref=dst, send_sem=send, recv_sem=recv, device_id=to, device_id_type=MESH
        )

    def lo_copy(j):
        rows = pl.ds(pl.multiple_of(j * CHUNK, CHUNK), CHUNK)
        return remote(raw.at[1 - first, rows, :], raw.at[1, rows, :], lo_send.at[j], lo_recv.at[j], lo_to)

    def hi_copy(j):
        rows = pl.ds(pl.multiple_of(HALF + j * CHUNK, CHUNK), CHUNK)
        return remote(raw.at[1 - last, rows, :], raw.at[1, rows, :], hi_send.at[j], hi_recv.at[j], hi_to)

    def start_lo(j, _):
        lo_copy(j).start()
        return 0

    def start_hi(j, _):
        hi_copy(j).start()
        return 0

    piece = pl.ds(pl.multiple_of(core * HALF + (v * 4 + u) * 32, 32), 32)

    def slab(g, rows):
        if g < 3:
            return wts.at[g + 1, pl.ds(0, 3), rows, :]
        return wts.at[pl.ds(1, 3), 3, rows, :]

    two_sec = jnp.where(core == 0, two_up[0], two_down[0])
    two_seq = jnp.where(core == 0, two_up[1], two_down[1])
    z_to = [down, (two_sec, two_seq), up]
    z_copies = [
        remote(wts.at[0, pl.ds(0, 3), piece, :], wts.at[r + 1, pl.ds(0, 3), piece, :], z_send.at[r], z_recv.at[r], z_to[r])
        for r in range(3)
    ] + [
        remote(wts.at[0, 3, piece, :], wts.at[r + 1, 3, piece, :], z_send.at[3 + r], z_recv.at[3 + r], z_to[r])
        for r in range(3)
    ]
    for copy in z_copies:
        copy.start()
    for copy in tok_loads:
        copy.wait()

    @pl.when(sec == 0)
    def _():
        lax.fori_loop(0, AHEAD, start_lo, 0)

    @pl.when(sec == 3)
    def _():
        lax.fori_loop(0, AHEAD, start_hi, 0)

    def piece_rows(u1, start=0, size=32):
        return pl.ds(pl.multiple_of(core * HALF + (v * 4 + u1) * 32 + start, 16), size)

    def row_copy(g, d):
        if d < 2:
            rows = piece_rows(u)
        elif d == 2:
            rows = piece_rows((u + 3) % 4, 0, 16)
        else:
            rows = piece_rows((u + 1) % 4, 16, 16)
        return remote(slab(g, rows), slab(g, rows), row_send.at[g * 4 + d], row_recv.at[g * 4 + d], row_to[d % 2])

    def set_rows(v1, start=0, size=128):
        return pl.ds(pl.multiple_of(core * HALF + v1 * 128 + start, 32), size)

    def col_copy(g, d):
        if d < 2:
            rows = set_rows(v)
        elif d == 2:
            rows = set_rows((v + 3) % 4, 0, 64)
        else:
            rows = set_rows((v + 1) % 4, 64, 64)
        return remote(slab(g, rows), slab(g, rows), col_send.at[g * 4 + d], col_recv.at[g * 4 + d], col_to[d % 2])

    def pair_copy(g, d):
        rows = set_rows((v + d) % 4)
        return remote(slab(g, rows), slab(g, rows), pair_send.at[g * 4 + d], pair_recv.at[g * 4 + d], sibling)

    def e1(g):
        if g < 3:
            z_copies[g].wait_recv()
        else:
            for r in range(3):
                z_copies[3 + r].wait_recv()
        for d in range(2):
            row_copy(g, d).start()

    def e2(g):
        for d in range(2):
            row_copy(g, d).wait_recv()
            row_copy(g, 2 + d).start()

    def e3(g):
        for d in range(2):
            row_copy(g, 2 + d).wait_recv()
        for d in range(2):
            col_copy(g, d).start()
        pair_copy(g, 0).start()

    def e4(g):
        col_copy(g, 0).wait_recv()
        col_copy(g, 2).start()
        pair_copy(g, 3).start()
        col_copy(g, 1).wait_recv()
        col_copy(g, 3).start()
        pair_copy(g, 1).start()

    def e5(g):
        col_copy(g, 2).wait_recv()
        col_copy(g, 3).wait_recv()
        pair_copy(g, 2).start()

    def e6(g):
        for d in range(4):
            pair_copy(g, d).wait_recv()

    def halo_step(k):
        @pl.when((sec == 0) & (k + AHEAD < CHUNKS))
        def _():
            lo_copy(k + AHEAD).start()

        @pl.when((sec == 3) & (k + AHEAD < CHUNKS))
        def _():
            hi_copy(k + AHEAD).start()

        j = k - SKEW * (3 - sec)

        @pl.when((j >= 0) & (j < CHUNKS))
        def _():
            lo_copy(j).wait_recv()

            @pl.when(sec != 0)
            def _():
                lo_copy(j).start()

        i = k - SKEW * sec

        @pl.when((i >= 0) & (i < CHUNKS))
        def _():
            hi_copy(i).wait_recv()

            @pl.when(sec != 3)
            def _():
                hi_copy(i).start()

    def own_unit(r, t):
        rows = pl.ds(pl.multiple_of(t * 512, 512), 512)
        x = norm[0, rows, :]
        q = jnp.dot(x, wts[r, 0], preferred_element_type=F32)
        q_buf[r, rows, :] = (q * QSCALE).astype(BF16)
        own_kv[r, 0, rows, :] = jnp.dot(x, wts[r, 1], preferred_element_type=F32).astype(BF16)
        own_kv[r, 1, rows, :] = jnp.dot(x, wts[r, 2], preferred_element_type=F32).astype(BF16)

    def halo_unit(m, count, r):
        size = 128 * count
        low = pl.ds(m * 128, size)
        high = pl.ds(HALF + m * 128, size)
        x = jnp.concatenate([norm[1, low, :], norm[1, high, :]], axis=0)
        for w in range(2):
            y = jnp.dot(x, wts[r, 1 + w], preferred_element_type=F32).astype(BF16)
            halo_kv[w, r, low, :] = y[:size]
            halo_kv[w, r, high, :] = y[size:]

    def halo_all(m):
        for r in range(GROUP):
            halo_unit(m, 1, r)

    def own_stores(r):
        return [
            pltpu.make_async_copy(q_buf.at[r], q_out.at[r], store_sem.at[r * 2]),
            pltpu.make_async_copy(own_kv.at[r], kv_out.at[:, r, pl.ds(0, TOK), :], store_sem.at[r * 2 + 1]),
        ]

    def kv_copy(r):
        return remote(own_kv.at[r], kv_out.at[:, r, pl.ds(2 * TOK, TOK), :], kv_send.at[r], kv_recv.at[r], sibling)

    def halo_stores(m):
        copies = []
        for h in range(2):
            copies.append(
                pltpu.make_async_copy(
                    halo_kv.at[:, :, pl.ds(h * HALF + m * 128, 128), :],
                    kv_out.at[:, :, pl.ds(TOK + h * HALF + m * 128, 128), :],
                    hstore_sem.at[m * 2 + h],
                )
            )
        return copies

    def finish_own(r):
        for copy in own_stores(r):
            copy.start()
        kv_copy(r).start()

    def run(first_step, last_step, events, unit):
        def body(k, _):
            halo_step(k)
            for at, event in events:
                pl.when(k == at)(event)
            unit(k)
            return 0

        lax.fori_loop(first_step, last_step + 1, body, 0)

    def seqn(*pairs):
        def go():
            for fn, g in pairs:
                fn(g)

        return go

    gain_load.wait()
    lax.fori_loop(0, TOK // 128, norm_own, 0)

    def unit_r0(k):
        @pl.when(k % 4 == 0)
        def _():
            own_unit(0, k // 4)

    run(0, 7, [(6, seqn((e1, 0), (e1, 1))), (7, seqn((e1, 2), (e1, 3)))], unit_r0)
    finish_own(0)
    run(
        8,
        27,
        [
            (10, seqn((e2, 0), (e2, 1))),
            (11, seqn((e2, 2))),
            (12, seqn((e2, 3))),
            (14, seqn((e3, 0))),
            (15, seqn((e3, 1))),
            (20, seqn((e4, 0), (e3, 2))),
            (23, seqn((e4, 1), (e3, 3))),
            (24, seqn((e5, 0))),
            (25, seqn((norm_halo, 0))),
        ],
        lambda k: None,
    )
    run(28, 32, [(28, seqn((e6, 0), (e4, 2))), (29, seqn((e5, 1))), (32, seqn((e6, 1), (e4, 3), (norm_halo, 1)))], lambda k: pl.when((k == 28) | (k == 30))(lambda: own_unit(1, (k - 28) // 2)))
    finish_own(1)

    def unit_r2(k):
        t = k - 33

        @pl.when(t % 2 == 0)
        def _():
            own_unit(2, t // 2)
            halo_unit(0, 2, t // 2)

    run(33, 36, [(34, seqn((e5, 2)))], unit_r2)
    finish_own(2)

    def unit_r3(k):
        t = k - 37

        @pl.when(t % 2 == 0)
        def _():
            own_unit(3, t // 2)
            halo_unit(0, 2, 2 + t // 2)

    run(37, 40, [(37, seqn((e6, 2))), (38, seqn((e5, 3)))], unit_r3)
    finish_own(3)
    run(
        41,
        STEPS - 1,
        [(42, seqn((norm_halo, 2))), (43, seqn((e6, 3)))],
        lambda k: pl.when(k == 43)(lambda: halo_all(2)),
    )
    norm_halo(3)
    wo_store = pltpu.make_async_copy(wts.at[:, 3], wo_out, wload_sem.at[7])
    wo_store.start()
    for m in range(3):
        for copy in halo_stores(m):
            copy.start()

    halo_all(3)
    for copy in halo_stores(3):
        copy.start()

    def drain(j, _):
        lo_copy(j).wait_send()
        hi_copy(j).wait_send()
        return 0

    lax.fori_loop(0, CHUNKS, drain, 0)
    for copy in z_copies:
        copy.wait_send()
    for g in range(4):
        for d in range(4):
            row_copy(g, d).wait_send()
            col_copy(g, d).wait_send()
            pair_copy(g, d).wait_send()
    for r in range(GROUP):
        for copy in own_stores(r):
            copy.wait()
        kv_copy(r).wait()
    wo_store.wait()
    for m in range(4):
        for copy in halo_stores(m):
            copy.wait()


def project(tokens, gain, wq, wk, wv, wo):
    any_spec = pl.BlockSpec(memory_space=pltpu.HBM)
    dma = pltpu.SemaphoreType.DMA
    return pl.pallas_call(
        gather_project,
        out_shape=[
            jax.ShapeDtypeStruct((GROUP, TOK, COLS), BF16),
            jax.ShapeDtypeStruct((2, GROUP, 3 * TOK, COLS), BF16),
            jax.ShapeDtypeStruct((GROUP, WIDTH, COLS), BF16),
        ],
        in_specs=[any_spec] * 6,
        out_specs=[any_spec] * 3,
        scratch_shapes=[
            pltpu.VMEM((1, WIDTH), F32),
            pltpu.VMEM((2, TOK, WIDTH), BF16),
            pltpu.VMEM((2, TOK, WIDTH), BF16),
            pltpu.VMEM((GROUP, 4, WIDTH, COLS), BF16),
            pltpu.VMEM((GROUP, TOK, COLS), BF16),
            pltpu.VMEM((GROUP, 2, TOK, COLS), BF16),
            pltpu.VMEM((2, GROUP, TOK, COLS), BF16),
            dma, dma((4,)), dma((8,)),
            dma((CHUNKS,)), dma((CHUNKS,)), dma((CHUNKS,)), dma((CHUNKS,)),
            dma((6,)), dma((6,)), dma((16,)), dma((16,)), dma((16,)), dma((16,)), dma((16,)), dma((16,)),
            dma((4,)), dma((4,)), dma((8,)), dma((8,)),
        ],
        compiler_params=pltpu.CompilerParams(
            collective_id=0, has_side_effects=True, vmem_limit_bytes=62 * 2**20
        ),
        name="gather_project",
    )(tokens, gain, wq, wk, wv, wo)


PAIRS = 4
LAG = 4
ROWS = 1024


def attend_decode(
    near_ref, counts_ref, stain_ref, q_hbm, kv_hbm, wo_hbm, tok_hbm, gain_ref, sw_hbm,
    out_hbm,
    q_buf, k_buf, v_buf, wo_buf, tok_buf, sw_buf, att, e_scr, out_buf,
    q_sem, k_sem, v_sem, late_sem, out_sem,
):
    seq = lax.axis_index("seq")
    blocks = TOK // BLOCK
    stain = stain_ref[0]

    def loads(r):
        return [
            pltpu.make_async_copy(q_hbm.at[r], q_buf.at[r], q_sem.at[r]),
            pltpu.make_async_copy(kv_hbm.at[0, r], k_buf.at[r], k_sem.at[r]),
            pltpu.make_async_copy(kv_hbm.at[1, r], v_buf.at[r], v_sem.at[r]),
        ]

    late = [
        pltpu.make_async_copy(wo_hbm, wo_buf, late_sem.at[0]),
        pltpu.make_async_copy(tok_hbm, tok_buf, late_sem.at[1]),
        pltpu.make_async_copy(sw_hbm.at[stain], sw_buf, late_sem.at[2]),
    ]
    for r in range(GROUP):
        for copy in loads(r):
            copy.start()
    for copy in late:
        copy.start()

    def place(near):
        owner = near // blocks - seq
        part = jnp.where(owner == 0, 0, jnp.where(owner == 2 * (seq % 2) - 1, 1, 2))
        return pl.multiple_of((part * blocks + near % blocks) * BLOCK, BLOCK)

    lane = lax.broadcasted_iota(jnp.int32, (BLOCK, BLOCK), 1)

    def block(i, h):
        rows = pl.ds(pl.multiple_of(i * BLOCK, BLOCK), BLOCK)
        starts = [place(near_ref[i, j]) for j in range(NEIGH)]

        def score(p, n):
            r, c = 2 * h + p // 2, (p % 2) * BLOCK
            q = q_buf[r, rows, c : c + BLOCK]
            zero = jnp.zeros_like(q)
            both = jnp.concatenate([jnp.where(lane < HEAD_DIM, q, zero), jnp.where(lane < HEAD_DIM, zero, q)], axis=0)
            k = jnp.concatenate([k_buf[r, pl.ds(starts[j], BLOCK), c : c + BLOCK] for j in range(n)], axis=0)
            s = lax.dot_general(both, k, (((1,), (1,)), ((), ())), preferred_element_type=F32)
            top = jnp.max(s, axis=1, keepdims=True)
            e_scr[p, :, : n * BLOCK] = jnp.exp2(s - top).astype(BF16)

        def mix(p, n):
            r, c = 2 * h + p // 2, (p % 2) * BLOCK
            v = jnp.concatenate([v_buf[r, pl.ds(starts[j], BLOCK), c : c + BLOCK] for j in range(n)], axis=0)
            v = jnp.concatenate([v, jnp.ones((n * BLOCK, BLOCK), BF16)], axis=1)
            o = jnp.dot(e_scr[p, :, : n * BLOCK], v, preferred_element_type=F32)
            o = o[:, :BLOCK] / o[:, BLOCK:]
            att[r, rows, c : c + BLOCK] = jnp.where(lane < HEAD_DIM, o[:BLOCK], o[BLOCK:]).astype(BF16)

        def run(n):
            for t in range(PAIRS + LAG):
                if t < PAIRS:
                    score(t, n)
                if t >= LAG:
                    mix(t - LAG, n)

        for n in range(3, NEIGH + 1):
            pl.when(counts_ref[i] == n)(functools.partial(run, n))

    def half(h, _):
        for r in range(2):
            for copy in loads(2 * h + r):
                copy.wait()

        def one(i, _):
            block(i, h)
            return 0

        lax.fori_loop(0, blocks, one, 0)
        return 0

    lax.fori_loop(0, GROUP // 2, half, 0)

    for copy in late:
        copy.wait()
    gain = gain_ref[pl.ds(stain, 1), :]

    def store(t):
        rows = pl.ds(t * ROWS, ROWS)
        return pltpu.make_async_copy(out_buf.at[rows, :], out_hbm.at[0, rows, :], out_sem.at[t])

    def rows_out(t, _):
        rows = pl.ds(pl.multiple_of(t * ROWS, ROWS), ROWS)
        x = jnp.concatenate([att[r, rows, :] for r in range(GROUP)], axis=1)
        parts = []
        for c in range(GROUP):
            w = jnp.concatenate([wo_buf[r, c * COLS : (c + 1) * COLS, :] for r in range(GROUP)], axis=0)
            parts.append(jnp.dot(x, w, preferred_element_type=F32))
        mixed = jnp.concatenate(parts, axis=1)
        encoded = (tok_buf[rows, :].astype(F32) + mixed).astype(BF16).astype(F32)
        scale = lax.rsqrt(jnp.mean(encoded * encoded, axis=-1, keepdims=True) + 1e-05)
        decoded = (encoded * scale * gain).astype(BF16)
        out_buf[rows, :] = jnp.dot(decoded, sw_buf[...], preferred_element_type=F32).astype(BF16)
        store(t).start()
        return 0

    lax.fori_loop(0, TOK // ROWS, rows_out, 0)
    for t in range(TOK // ROWS):
        store(t).wait()


def attention(neighbours, counts, stain, q, kv, wo, tokens, stain_gain, stain_weight):
    hbm = pl.BlockSpec(memory_space=pltpu.HBM)
    smem = pl.BlockSpec(memory_space=pltpu.SMEM)
    dma = pltpu.SemaphoreType.DMA
    return pl.pallas_call(
        attend_decode,
        out_shape=jax.ShapeDtypeStruct((1, TOK, PIX), BF16),
        in_specs=[smem] * 3 + [hbm] * 4 + [pl.BlockSpec(memory_space=pltpu.VMEM), hbm],
        out_specs=hbm,
        scratch_shapes=[
            pltpu.VMEM((GROUP, TOK, COLS), BF16),
            pltpu.VMEM((GROUP, 3 * TOK, COLS), BF16),
            pltpu.VMEM((GROUP, 3 * TOK, COLS), BF16),
            pltpu.VMEM((GROUP, WIDTH, COLS), BF16),
            pltpu.VMEM((TOK, WIDTH), BF16),
            pltpu.VMEM((WIDTH, PIX), BF16),
            pltpu.VMEM((GROUP, TOK, COLS), BF16),
            pltpu.VMEM((PAIRS, 2 * BLOCK, NEIGH * BLOCK), BF16),
            pltpu.VMEM((TOK, PIX), BF16),
            dma((GROUP,)), dma((GROUP,)), dma((GROUP,)), dma((3,)), dma((TOK // ROWS,)),
        ],
        compiler_params=pltpu.CompilerParams(vmem_limit_bytes=62 * 2**20),
        name="attend_decode",
    )(neighbours, counts, stain, q, kv, wo, tokens, stain_gain, stain_weight)


def per_device(
    tokens, enc_gain, w_query, w_key, w_value, w_out, neighbours, counts, stain_of_section, stain_gain, stain_weight
):
    q, kv, wo = project(tokens, enc_gain[None, :], w_query, w_key, w_value, w_out)
    return attention(neighbours, counts, stain_of_section, q, kv, wo, tokens, stain_gain, stain_weight)


def solution(mesh):
    placed = (
        P("seq", None),
        P(),
        P(None, "section"),
        P(None, "section"),
        P(None, "section"),
        P("section", None),
        P("seq", None),
        P("seq"),
        P("section"),
        P(),
        P(),
    )
    return jax.shard_map(
        per_device, mesh=mesh, in_specs=placed, out_specs=P("section", "seq", None), check_vma=False
    )
```
